512 devices in a mesh: grp: 32 (over z, core), pan: 16 (over y, x).
Axes of the slice: x: 4, y: 4, z: 16, core: 2. Of those that a mesh axis runs over, the one named last changes fastest.
Arguments:
- jblocks: bfloat16 [196608, 4096], P(('grp', 'pan')), may hold values from -240 to 240
- blk_row: int32 [196608], P(('grp', 'pan')), may hold values from 0 to 3
- blk_src: int32 [196608], P(('grp', 'pan')), may hold values from 0 to 31, as said below
- blk_slot: int32 [196608], P(('grp', 'pan')), may hold values from 0 to 7, as said below
- live_count: int32 [512], P(('grp', 'pan')), may hold values from 256 to 384, as said below
- send_list: int32 [32, 16, 32, 8], P('grp', 'pan'), may hold values from 0 to 31, as said below
- omega: bfloat16 [1048576, 128], P(('grp', 'pan')), may hold values from -6 to 6
Outputs:
- projected: bfloat16 [1048576, 128], P(('grp', 'pan'))
The draws below stay inside these ranges and needn't reach their ends.
Inputs may be any that keep to these rules, and one draw needn't show every extreme that they name: `send_list`: within one row (owner, pan index, group) the 8 entries are distinct. On every device the first 256 stored blocks name each pair (blk_src, blk_slot) exactly once, in the order blk_src * 8 + blk_slot. `blk_slot`: see blk_src. `live_count`: some device has all 384 blocks live and some has only 256.
All inputs are finite; a program needn't handle non-finite values.
Results may differ from the reference program's by a relative error of at most 0.0012.
Values may be sent and summed in bfloat16 or wider, within the bound.
A program may use at most 128 MiB of HBM per device.

```python
import jax
import jax.numpy as jnp
from jax import lax

BLOCK = 64
WIDTH = 128
RB_DEV = 4
CB_DEV = 32
NB = 384
CAP = 8
NC = 1048576
N_GRP = 32
N_PAN = 16


def block_layout(key):
    devices = N_GRP * N_PAN
    extra = jax.random.randint(jax.random.fold_in(key, 11), (devices, NB - N_GRP * CAP), 0, N_GRP * CAP)
    covered = jnp.broadcast_to(jnp.arange(N_GRP * CAP, dtype=jnp.int32), (devices, N_GRP * CAP))
    return jnp.concatenate([covered, extra.astype(jnp.int32)], axis=1).reshape(-1)


def draw_blk_src(key, part):
    flat = block_layout(key)
    return (flat // CAP).astype(jnp.int32)


def draw_blk_slot(key, part):
    flat = block_layout(key)
    return (flat % CAP).astype(jnp.int32)


def draw_send_list(key, part):
    key = jax.random.fold_in(key, 3)
    scores = jax.random.randint(key, (N_GRP, N_PAN, N_GRP, CB_DEV), 0, 2 ** 20) * CB_DEV
    scores = scores + jnp.arange(CB_DEV, dtype=jnp.int32)
    scores = scores.at[0, 0, 0, CB_DEV - 1].set(-1)
    scores = scores.at[0, 0, 1, 0].set(-1)
    order = jnp.argsort(scores, axis=-1)
    return order[..., :CAP].astype(jnp.int32)


def draw_live_count(key, part):
    key = jax.random.fold_in(key, 5)
    first, second = jax.random.split(key)
    devices = N_GRP * N_PAN
    counts = jax.random.randint(first, (devices,), N_GRP * CAP, NB + 1)
    spots = jax.random.permutation(second, devices)
    counts = counts.at[spots[0]].set(NB)
    counts = counts.at[spots[1]].set(N_GRP * CAP)
    return counts.astype(jnp.int32)


def draw_jblocks(key, part):
    key = jax.random.fold_in(key, 7)
    first, second = jax.random.split(key)
    devices = N_GRP * N_PAN
    shape = (devices, NB, BLOCK * BLOCK)
    base = jnp.clip(jax.random.normal(first, shape, jnp.float32), -6.0, 6.0)
    spread = 0.5
    ramp = jnp.arange(devices, dtype=jnp.float32) / (devices - 1)
    jitter = jax.random.uniform(second, (devices, NB, 1), jnp.float32)
    scale = 4.0 * jnp.exp(2.302585 * (spread * ramp[:, None, None] + (1.0 - spread) * jitter))
    return (base * scale).reshape(devices * NB, BLOCK * BLOCK).astype(jnp.bfloat16)


def place_ends(result, stream_key, smallest, largest):
    dims = result.shape
    place = [jax.random.randint(jax.random.fold_in(stream_key, axis), (), 0, dims[axis]) for axis in range(len(dims))]
    result = result.at[tuple(place)].set(smallest)
    longest = dims.index(max(dims))
    place[longest] = (place[longest] + 1) % dims[longest]
    return result.at[tuple(place)].set(largest)


def steps_of(rng, extent, pieces, low, high):
    factor_of, own = 1.0, jax.random.fold_in(rng, 6)
    for position, blocks in pieces:
        draws = jnp.exp(jax.random.uniform(jax.random.fold_in(own, position), (blocks,), jnp.float32, low / len(pieces), high / len(pieces)))
        factor_of = factor_of * jnp.repeat(draws, extent[position] // blocks).reshape([-1 if axis == position else 1 for axis in range(len(extent))])
    return factor_of


def normal_values(key, shape, scale, bound, cuts=(), kind=jnp.bfloat16):
    array = scale * jax.random.normal(key, shape, jnp.float32)
    if cuts:
        array = array * steps_of(key, shape, cuts, -0.22, 0.18)
    return jnp.clip(array, -bound, bound).astype(kind)


def setup_inputs(seed: int = 0) -> dict:
    streams_of = jax.random.split(jax.random.key(seed), 8)
    jblocks = draw_jblocks(jax.random.fold_in(streams_of[7], 71), 0)
    blk_row = place_ends(jax.random.randint(streams_of[1], (NB * N_GRP * N_PAN,), 0, RB_DEV), jax.random.fold_in(streams_of[1], 1), 0, RB_DEV - 1).astype(jnp.int32)
    blk_src = draw_blk_src(jax.random.fold_in(streams_of[7], 71), 0)
    blk_slot = draw_blk_slot(jax.random.fold_in(streams_of[7], 71), 0)
    live_count = draw_live_count(jax.random.fold_in(streams_of[7], 71), 0)
    send_list = draw_send_list(jax.random.fold_in(streams_of[7], 71), 0)
    omega = normal_values(streams_of[6], (NC, WIDTH), 1.0, 6.0, ((0, 512),))
    return dict(jblocks=jblocks, blk_row=blk_row, blk_src=blk_src, blk_slot=blk_slot, live_count=live_count, send_list=send_list, omega=omega)


def reference(jblocks, blk_row, blk_src, blk_slot, live_count, send_list, omega):
    devices = N_GRP * N_PAN
    values = jblocks.reshape(devices, NB, BLOCK, BLOCK)
    live = jnp.arange(NB, dtype=jnp.int32)[None, :] < live_count[:, None]
    sources = blk_src.reshape(devices, NB)
    slot_ids = blk_slot.reshape(devices, NB)
    rows = blk_row.reshape(devices, NB)
    grp_ids = (jnp.arange(devices, dtype=jnp.int32) // N_PAN)[:, None]
    pan_ids = (jnp.arange(devices, dtype=jnp.int32) % N_PAN)[:, None]
    local_cell = send_list[sources, pan_ids, grp_ids, slot_ids]
    columns = ((sources * N_PAN + pan_ids) * CB_DEV + local_cell).astype(jnp.int32)
    omega_blocks = omega.reshape(devices * CB_DEV, BLOCK, WIDTH)
    row_ids = jnp.arange(RB_DEV, dtype=jnp.int32)

    def device_sketch(item):
        vals, alive, cols, rws = item
        mats = jnp.where(alive[:, None, None], vals.astype(jnp.float32), jnp.zeros((), jnp.float32))
        picked = omega_blocks[cols].astype(jnp.float32)
        prods = jnp.einsum('bij,bjk->bik', mats, picked, precision=lax.Precision.HIGHEST)
        table = (rws[None, :] == row_ids[:, None]).astype(jnp.float32)
        return jnp.einsum('rb,bik->rik', table, prods, precision=lax.Precision.HIGHEST).reshape(RB_DEV * BLOCK, WIDTH)
    sketch = lax.map(device_sketch, (values, live, columns, rows)).reshape(devices * RB_DEV * BLOCK, WIDTH)
    gram = jnp.dot(sketch.T, sketch, precision=lax.Precision.HIGHEST)
    lower = jnp.linalg.cholesky(gram)
    basis = lax.linalg.triangular_solve(lower, sketch.T, left_side=True, lower=True).T
    basis_blocks = basis.reshape(devices, RB_DEV, BLOCK, WIDTH)

    def add_device(total, item):
        vals, alive, cols, rws, own_rows = item
        mats = jnp.where(alive[:, None, None], vals.astype(jnp.float32), jnp.zeros((), jnp.float32))
        chosen = own_rows[rws]
        terms = jnp.einsum('bij,bik->bjk', mats, chosen, precision=lax.Precision.HIGHEST)
        return (total.at[cols].add(terms), None)
    start = jnp.zeros((devices * CB_DEV, BLOCK, WIDTH), jnp.float32)
    total, unused = lax.scan(add_device, start, (values, live, columns, rows, basis_blocks))
    return total.reshape(devices * CB_DEV * BLOCK, WIDTH).astype(jnp.bfloat16)
```

```python
import functools

import jax
import jax.numpy as jnp
from jax import lax
from jax.experimental import pallas as pl
from jax.experimental.pallas import tpu as pltpu
from jax.sharding import PartitionSpec as P

BLOCK = 64
RB_DEV = 4
PIECES = 2
MOST_GAIN = 8.0
MESH = pl.DeviceIdType.MESH
HIGHEST = lax.Precision.HIGHEST


def places(chips):
    g = lax.axis_index("grp")
    core = lax.rem(g, 2)
    z = (g - core) // 2
    up = lax.rem(z + 1, chips) * 2 + core
    down = lax.rem(z + chips - 1, chips) * 2 + core
    return g, core, z, up, down, g + 1 - 2 * core


def greet(others):
    barrier = pltpu.get_barrier_semaphore()
    for other in others:
        pl.semaphore_signal(barrier, inc=1, device_id={"grp": other}, device_id_type=MESH)
    pl.semaphore_wait(barrier, len(others))


def gather_kernel(
    chips, mine, listed, gathered, lists, keep, ring_send, ring_recv, side_send, side_recv, own_send, own_recv,
    list_send, list_recv, list_side_send, list_side_recv,
):
    g, core, z, up, down, side = places(chips)
    half = chips // 2
    step = mine.shape[0] // PIECES

    def rows(piece):
        return pl.ds(piece * step, step)

    def owner(way, hop):
        where = z + chips - hop if way == 0 else z + hop
        return lax.rem(where, chips) * 2 + core

    def ring(way, hop, piece, from_mine=False):
        at = owner(way, hop - 1)
        source = mine.at[rows(piece)] if from_mine else gathered.at[at, rows(piece)]
        return pltpu.make_async_remote_copy(
            src_ref=source,
            dst_ref=gathered.at[at, rows(piece)],
            send_sem=ring_send.at[way, hop - 1, piece],
            recv_sem=ring_recv.at[way, hop - 1, piece],
            device_id={"grp": up if way == 0 else down},
            device_id_type=MESH,
        )

    def arrival(way, hop, piece):
        at = owner(way, hop)
        return pltpu.make_async_remote_copy(
            src_ref=gathered.at[at, rows(piece)],
            dst_ref=gathered.at[at, rows(piece)],
            send_sem=ring_send.at[way, hop - 1, piece],
            recv_sem=ring_recv.at[way, hop - 1, piece],
            device_id={"grp": up if way == 0 else down},
            device_id_type=MESH,
        )

    def across(way, hop, piece, arriving=False):
        at = owner(way, hop) + (1 - 2 * core if arriving else 0)
        return pltpu.make_async_remote_copy(
            src_ref=gathered.at[at, rows(piece)],
            dst_ref=gathered.at[at, rows(piece)],
            send_sem=side_send.at[way, hop - 1, piece],
            recv_sem=side_recv.at[way, hop - 1, piece],
            device_id={"grp": side},
            device_id_type=MESH,
        )

    def own(piece, at):
        return pltpu.make_async_remote_copy(
            src_ref=mine.at[rows(piece)],
            dst_ref=gathered.at[at, rows(piece)],
            send_sem=own_send.at[piece],
            recv_sem=own_recv.at[piece],
            device_id={"grp": side},
            device_id_type=MESH,
        )

    def last(way):
        return range(PIECES // 2) if way == 0 else range(PIECES // 2, PIECES)

    def list_ring(way, hop):
        at = owner(way, hop - 1)
        return pltpu.make_async_remote_copy(
            src_ref=lists.at[at],
            dst_ref=lists.at[at],
            send_sem=list_send.at[way, hop - 1],
            recv_sem=list_recv.at[way, hop - 1],
            device_id={"grp": up if way == 0 else down},
            device_id_type=MESH,
        )

    def list_arrival(way, hop):
        at = owner(way, hop)
        return pltpu.make_async_remote_copy(
            src_ref=lists.at[at],
            dst_ref=lists.at[at],
            send_sem=list_send.at[way, hop - 1],
            recv_sem=list_recv.at[way, hop - 1],
            device_id={"grp": up if way == 0 else down},
            device_id_type=MESH,
        )

    def list_across(way, hop, arriving=False):
        at = owner(way, hop) + (1 - 2 * core if arriving else 0)
        return pltpu.make_async_remote_copy(
            src_ref=lists.at[at],
            dst_ref=lists.at[at],
            send_sem=list_side_send.at[way, hop],
            recv_sem=list_side_recv.at[way, hop],
            device_id={"grp": side},
            device_id_type=MESH,
        )

    greet((up, down, side))
    kept = pltpu.make_async_copy(mine, gathered.at[g], keep.at[0])
    kept.start()
    listing = pltpu.make_async_copy(listed, lists.at[g], keep.at[1])
    listing.start()
    listing.wait()
    list_ring(0, 1).start()
    list_ring(1, 1).start()
    list_across(0, 0).start()
    for piece in range(PIECES):
        for way in range(2):
            ring(way, 1, piece, True).start()
    for piece in range(PIECES):
        own(piece, g).start()

    def pass_on(hop, carry):
        for way in range(2):
            list_arrival(way, hop).wait_recv()
            list_ring(way, hop + 1).start()
            list_across(way, hop).start()
        for piece in range(PIECES):
            for way in range(2):
                arrival(way, hop, piece).wait_recv()
                ring(way, hop + 1, piece).start()
                across(way, hop, piece).start()
        return carry

    lax.fori_loop(1, half - 1, pass_on, 0)
    for way in range(2):
        list_arrival(way, half - 1).wait_recv()
        list_across(way, half - 1).start()
    list_ring(0, half).start()
    list_arrival(0, half).wait_recv()
    list_across(0, half).start()
    for piece in range(PIECES):
        for way in range(2):
            arrival(way, half - 1, piece).wait_recv()
            if piece in last(way):
                ring(way, half, piece).start()
            across(way, half - 1, piece).start()
    for way in range(2):
        for piece in last(way):
            arrival(way, half, piece).wait_recv()
            across(way, half, piece).start()

    for piece in range(PIECES):
        ring(0, 1, piece, True).wait_send()
        ring(1, 1, piece, True).wait_send()
        own(piece, g).wait_send()
        own(piece, side).wait_recv()

    list_across(0, 0).wait_send()
    list_across(0, 0, True).wait_recv()
    list_ring(0, half).wait_send()
    list_across(0, half).wait_send()
    list_across(0, half, True).wait_recv()

    def finish_lists(hop, carry):
        for way in range(2):
            list_ring(way, hop).wait_send()
            list_across(way, hop).wait_send()
            list_across(way, hop, True).wait_recv()
        return carry

    lax.fori_loop(1, half, finish_lists, 0)

    def finish(hop, carry):
        for piece in range(PIECES):
            for way in range(2):
                ring(way, hop + 1, piece).wait_send()
                across(way, hop, piece).wait_send()
                across(way, hop, piece, True).wait_recv()
        return carry

    lax.fori_loop(1, half - 1, finish, 0)
    for piece in range(PIECES):
        for way in range(2):
            if piece in last(way):
                ring(way, half, piece).wait_send()
            across(way, half - 1, piece).wait_send()
            across(way, half - 1, piece, True).wait_recv()
    for way in range(2):
        for piece in last(way):
            across(way, half, piece).wait_send()
            across(way, half, piece, True).wait_recv()
    kept.wait()


def gather(chips, omega, listed):
    rows, width = omega.shape
    half = chips // 2
    dma = pltpu.SemaphoreType.DMA
    hbm = pl.BlockSpec(memory_space=pl.ANY)
    return pl.pallas_call(
        functools.partial(gather_kernel, chips),
        out_shape=[
            jax.ShapeDtypeStruct((2 * chips, rows, width), omega.dtype),
            jax.ShapeDtypeStruct((2 * chips,) + listed.shape, listed.dtype),
        ],
        in_specs=[hbm, hbm],
        out_specs=[hbm, hbm],
        scratch_shapes=[dma((2,))]
        + [dma((2, half, PIECES))] * 4
        + [dma((PIECES,))] * 2
        + [dma((2, half))] * 2
        + [dma((2, half + 1))] * 2,
        compiler_params=pltpu.CompilerParams(collective_id=0, has_side_effects=True),
    )(omega, listed)


def local_kernel(
    first, lists, blk_row, blk_src, blk_slot, live, x, cells, parts, gram, my_at, their_at, sketch, halves
):
    lane = lax.broadcasted_iota(jnp.int32, (1, 2 * BLOCK), 1)
    blocks = x.shape[0]
    owners, cap = lists.shape[0], lists.shape[1]
    g = lax.axis_index("grp")
    core = lax.rem(g, 2)
    here = lax.broadcasted_iota(jnp.int32, (1, my_at.shape[1]), 1)

    def row_of(at):
        return jnp.where(at < live[0], blk_row[at], -1)

    def slot_of(at):
        return blk_src[at] * cap + blk_slot[at]

    def place(owner, carry):
        mine = jnp.full(here.shape, owners * cap, jnp.int32)
        theirs = jnp.full(here.shape, owners // 2 * cap, jnp.int32)
        for n in range(cap):
            mine = jnp.where(here == lists[owner, n, g], owner * cap + n, mine)
            theirs = jnp.where(here == lists[owner, n, g + 1 - 2 * core], owner // 2 * cap + n, theirs)
        my_at[pl.ds(owner, 1), :] = mine
        their_at[pl.ds(owner, 1), :] = theirs
        return carry

    lax.fori_loop(0, owners, place, 0)

    def pair_of(at):
        a, b = x[at], x[at + 1]
        even = jnp.concatenate([a[:, :BLOCK], b[:, :BLOCK]], axis=1)
        odd = jnp.concatenate([a[:, BLOCK:], b[:, BLOCK:]], axis=1)
        both = jnp.concatenate([even, odd], axis=0)
        rows = jnp.where(lane < BLOCK, row_of(at), row_of(at + 1))
        return jnp.concatenate(
            [both * jnp.where(rows == r, 1.0, 0.0).astype(both.dtype) for r in range(RB_DEV)], axis=0
        )

    def four_of(at):
        return jnp.concatenate([pair_of(at), pair_of(at + 2)], axis=1)

    def cell_rows(at):
        first_row = lists[blk_src[at], blk_slot[at], g] * BLOCK
        return cells[blk_src[at], pl.ds(pl.multiple_of(first_row, BLOCK), BLOCK), :]

    sketch[...] = jnp.zeros_like(sketch)

    def forward(i, carry):
        at = i * 4
        picked = jnp.concatenate([cell_rows(at + n) for n in range(4)], axis=0)
        sketch[...] += jnp.dot(four_of(at), picked, preferred_element_type=jnp.float32)
        return carry

    lax.fori_loop(0, blocks // 4, forward, 0)
    s = sketch[...]
    gram[...] = lax.dot_general(
        s, s, (((0,), (0,)), ((), ())), precision=HIGHEST, preferred_element_type=jnp.float32
    )
    high = s.astype(jnp.bfloat16)
    low = (s - high.astype(jnp.float32)).astype(jnp.bfloat16)
    halves[...] = jnp.concatenate([high, low], axis=1)
    width = s.shape[1]

    def back(at):
        two = lax.dot_general(
            four_of(at), halves[...], (((0,), (0,)), ((), ())), preferred_element_type=jnp.float32
        )
        return two[:, :width] + two[:, width:]

    def base(i, carry):
        out = back(i * 4)
        for n in range(4):
            parts[i * 4 + n] = out[n * BLOCK : (n + 1) * BLOCK]
        return carry

    lax.fori_loop(0, first // 4, base, 0)
    parts[first] = jnp.zeros((BLOCK, width), jnp.float32)

    def extra(i, carry):
        out = back(i * 4)
        for n in range(4):
            parts[slot_of(i * 4 + n)] += out[n * BLOCK : (n + 1) * BLOCK]
        return carry

    lax.fori_loop(first // 4, blocks // 4, extra, 0)


def local(first, lists, blk_row, blk_src, blk_slot, live, x, cells):
    width = cells.shape[-1]
    owners = cells.shape[0]
    smem = pl.BlockSpec(memory_space=pltpu.SMEM)
    vmem = pl.BlockSpec(memory_space=pltpu.VMEM)
    return pl.pallas_call(
        functools.partial(local_kernel, first),
        out_shape=[
            jax.ShapeDtypeStruct((first + 1, BLOCK, width), jnp.float32),
            jax.ShapeDtypeStruct((width, width), jnp.float32),
            jax.ShapeDtypeStruct((owners, width), jnp.int32),
            jax.ShapeDtypeStruct((owners, width), jnp.int32),
        ],
        in_specs=[smem, smem, smem, smem, smem, vmem, vmem],
        out_specs=[vmem] * 4,
        scratch_shapes=[
            pltpu.VMEM((RB_DEV * BLOCK, width), jnp.float32),
            pltpu.VMEM((RB_DEV * BLOCK, 2 * width), jnp.bfloat16),
        ],
        compiler_params=pltpu.CompilerParams(vmem_limit_bytes=56 * 1024 * 1024),
    )(lists, blk_row, blk_src, blk_slot, live, x, cells)


def return_kernel(
    chips, cap, parts, mine, theirs, out, other, sent, got, sent_scale, got_scale,
    side_send, side_recv, ring_send, ring_recv, scale_send, scale_recv,
):
    g, core, z, up, down, side = places(chips)
    half = chips // 2
    count = out.shape[0]
    size = count // PIECES
    greet((up, down, side))

    def chip(n):
        return lax.rem(z + n, chips)

    def across(n):
        at = chip(n)
        return pltpu.make_async_remote_copy(
            src_ref=parts.at[pl.ds((at * 2 + 1 - core) * cap, cap)],
            dst_ref=other.at[pl.ds(at * cap, cap)],
            send_sem=side_send.at[n],
            recv_sem=side_recv.at[n],
            device_id={"grp": side},
            device_id_type=MESH,
        )

    def blocks(piece):
        return pl.ds(piece * size, size)

    def ring(way, hop, piece):
        to = {"grp": up if way == 0 else down}
        values = pltpu.make_async_remote_copy(
            src_ref=sent.at[way, hop, blocks(piece)],
            dst_ref=got.at[way, hop, blocks(piece)],
            send_sem=ring_send.at[way, hop, piece],
            recv_sem=ring_recv.at[way, hop, piece],
            device_id=to,
            device_id_type=MESH,
        )
        scales = pltpu.make_async_remote_copy(
            src_ref=sent_scale.at[way, hop, blocks(piece)],
            dst_ref=got_scale.at[way, hop, blocks(piece)],
            send_sem=scale_send.at[way, hop, piece],
            recv_sem=scale_recv.at[way, hop, piece],
            device_id=to,
            device_id_type=MESH,
        )
        return values, scales

    lax.fori_loop(0, chips, lambda n, c: (across(n).start(), c)[1], 0)
    other[other.shape[0] - 1] = jnp.zeros(out.shape[1:], jnp.float32)
    lax.fori_loop(0, chips, lambda n, c: (across(n).wait_recv(), c)[1], 0)

    def own(target, q):
        owner = target * 2 + core
        return parts[mine[owner, q]] + other[theirs[owner, q]]

    def read(way, hop, q):
        return got[way, hop, q].astype(jnp.int32).astype(jnp.float32) * got_scale[way, hop, pl.ds(q, 1), :]

    def await_piece(way, hop, piece):
        for copy in ring(way, hop, piece):
            copy.wait_recv()

    def send(way, hop, piece, onward):
        target = chip(half - hop if way == 0 else chips - half + hop)
        if onward:
            await_piece(way, hop - 1, piece)

        def block(q, carry):
            total = own(target, q)
            if onward:
                total = total + read(way, hop - 1, q)
            top = jnp.max(jnp.abs(total), axis=0, keepdims=True)
            usable = top > 1e-30
            factor = jnp.where(usable, 32767.0 / jnp.where(usable, top, 1.0), 0.0)
            sent[way, hop, q] = jnp.round(total * factor).astype(jnp.int32).astype(jnp.int16)
            sent_scale[way, hop, pl.ds(q, 1), :] = top * (1.0 / 32767.0)
            return carry

        lax.fori_loop(piece * size, (piece + 1) * size, block, 0)
        for copy in ring(way, hop, piece):
            copy.start()

    def first(way):
        return range(PIECES // 2) if way == 0 else range(PIECES // 2, PIECES)

    for way in range(2):
        for piece in first(way):
            send(way, 0, piece, False)
    for piece in range(PIECES):
        for way in range(2):
            send(way, 1, piece, piece in first(way))

    def onward(hop, carry):
        for piece in range(PIECES):
            for way in range(2):
                send(way, hop, piece, True)
        return carry

    lax.fori_loop(2, half, onward, 0)
    for piece in range(PIECES):
        for way in range(2):
            await_piece(way, half - 1, piece)

        def block(q, carry):
            out[q] = own(z, q) + read(0, half - 1, q) + read(1, half - 1, q)
            return carry

        lax.fori_loop(piece * size, (piece + 1) * size, block, 0)

    def finish(way, hop, piece):
        for copy in ring(way, hop, piece):
            copy.wait_send()

    for way in range(2):
        for piece in first(way):
            finish(way, 0, piece)

    def finish_all(hop, carry):
        for piece in range(PIECES):
            for way in range(2):
                finish(way, hop, piece)
        return carry

    lax.fori_loop(1, half, finish_all, 0)
    lax.fori_loop(0, chips, lambda n, c: (across(n).wait_send(), c)[1], 0)


def give_back(chips, cap, count, parts, mine, theirs):
    edge, width = parts.shape[1:]
    half = chips // 2
    dma = pltpu.SemaphoreType.DMA
    smem = pl.BlockSpec(memory_space=pltpu.SMEM)
    vmem = pl.BlockSpec(memory_space=pltpu.VMEM)
    return pl.pallas_call(
        functools.partial(return_kernel, chips, cap),
        out_shape=jax.ShapeDtypeStruct((count, edge, width), jnp.float32),
        in_specs=[vmem, smem, smem],
        out_specs=vmem,
        scratch_shapes=[
            pltpu.VMEM((chips * cap + 1, edge, width), jnp.float32),
            pltpu.VMEM((2, half, count, edge, width), jnp.int16),
            pltpu.VMEM((2, half, count, edge, width), jnp.int16),
            pltpu.VMEM((2, half, count, width), jnp.float32),
            pltpu.VMEM((2, half, count, width), jnp.float32),
            dma((chips,)),
            dma((chips,)),
            dma((2, half, PIECES)),
            dma((2, half, PIECES)),
            dma((2, half, PIECES)),
            dma((2, half, PIECES)),
        ],
        compiler_params=pltpu.CompilerParams(
            collective_id=1, has_side_effects=True, vmem_limit_bytes=56 * 1024 * 1024
        ),
    )(parts, mine, theirs)


def finish_kernel(gram, z, out, gain, a, v):
    n = gram.shape[0]
    lane = lax.broadcasted_iota(jnp.int32, (n, n), 1)
    sub = lax.broadcasted_iota(jnp.int32, (n, n), 0)
    a[...] = gram[...]
    v[...] = jnp.where(lane == sub, 1.0, 0.0)

    def pivot(j, carry):
        old = a[...]
        row_a, row_v = a[pl.ds(j, 1), :], v[pl.ds(j, 1), :]
        d = jnp.sum(jnp.where(lane[:1] == j, row_a, 0.0), axis=1, keepdims=True)
        column = jnp.sum(jnp.where(lane == j, old, 0.0), axis=1, keepdims=True)
        factor = jnp.where(sub > j, column / d, 0.0)
        a[...] = old - factor * row_a
        v[...] = v[...] - factor * row_v
        return carry

    lax.fori_loop(0, n, pivot, 0)
    d = jnp.sum(jnp.where(lane == sub, a[...], 0.0), axis=1, keepdims=True)
    inverse = v[...] / jnp.sqrt(d)
    spread = jnp.sum(jnp.where(lane == sub, gram[...], 0.0), axis=0, keepdims=True)
    grown = jnp.sum(inverse * inverse * spread, axis=1, keepdims=True)
    gain[...] = jnp.broadcast_to(jnp.sum(grown, axis=0, keepdims=True), gain.shape)
    high = inverse.astype(jnp.bfloat16)
    low = (inverse - high.astype(jnp.float32)).astype(jnp.bfloat16)
    factors = jnp.concatenate(
        [
            jnp.concatenate([high, high], axis=1),
            jnp.concatenate([low, jnp.zeros_like(low)], axis=1),
        ],
        axis=0,
    )

    def rows(i, carry):
        at = pl.ds(pl.multiple_of(i * 256, 256), 256)
        value = z[at, :]
        top = value.astype(jnp.bfloat16)
        rest = (value - top.astype(jnp.float32)).astype(jnp.bfloat16)
        two = lax.dot_general(
            jnp.concatenate([top, rest], axis=1), factors, (((1,), (1,)), ((), ())),
            preferred_element_type=jnp.float32,
        )
        out[at, :] = (two[:, :n] + two[:, n:]).astype(out.dtype)
        return carry

    lax.fori_loop(0, z.shape[0] // 256, rows, 0)


def finish(gram, z):
    n = gram.shape[0]
    vmem = pl.BlockSpec(memory_space=pltpu.VMEM)
    return pl.pallas_call(
        finish_kernel,
        out_shape=[
            jax.ShapeDtypeStruct(z.shape, jnp.bfloat16),
            jax.ShapeDtypeStruct((8, n), jnp.float32),
        ],
        in_specs=[vmem, vmem],
        out_specs=[vmem, vmem],
        scratch_shapes=[pltpu.VMEM((n, n), jnp.float32), pltpu.VMEM((n, n), jnp.float32)],
    )(gram, z)


def factor_of(sketch):
    local_gram = jnp.dot(sketch.T, sketch, precision=lax.Precision.HIGHEST)
    gram = lax.psum(local_gram, ("grp", "pan"))
    return jnp.linalg.cholesky(gram)


def careful(jblocks, blk_row, blk_src, blk_slot, live_count, send_list, omega):
    block_count = jblocks.shape[0]
    width = omega.shape[1]
    groups = lax.axis_size("grp")
    lists = send_list.reshape(-1)
    slots = lists.shape[0]
    cap = slots // groups
    edge = BLOCK
    cell_blocks = omega.shape[0] // edge
    alive = jnp.arange(block_count, dtype=jnp.int32) < live_count[0]
    values = jnp.where(alive[:, None], jblocks, jnp.zeros((), jblocks.dtype)).reshape(
        block_count, edge, edge
    )
    omega_blocks = omega.reshape(cell_blocks, edge, width)
    outgoing = jnp.take(omega_blocks, lists, axis=0).reshape(groups, cap * edge, width)
    incoming = lax.all_to_all(outgoing, "grp", split_axis=0, concat_axis=0, tiled=True).reshape(
        slots, edge, width
    )
    slot_index = blk_src * cap + blk_slot
    picked = jnp.take(incoming, slot_index, axis=0)
    products = jnp.einsum("bij,bjk->bik", values, picked, preferred_element_type=jnp.float32)
    sketch = jax.ops.segment_sum(products, blk_row, num_segments=RB_DEV)
    sketch = sketch.reshape(RB_DEV * edge, width)
    lower = factor_of(sketch)
    used_rows = lax.linalg.triangular_solve(lower, sketch.T, left_side=True, lower=True).T
    chosen = jnp.take(used_rows.reshape(RB_DEV, edge, width), blk_row, axis=0)
    terms = jnp.einsum(
        "bij,bik->bjk",
        values.astype(jnp.float32),
        chosen,
        precision=lax.Precision.HIGH,
        preferred_element_type=jnp.float32,
    )
    per_slot = terms[:slots].at[slot_index[slots:]].add(terms[slots:])
    returned = lax.all_to_all(
        per_slot.reshape(groups, cap * edge, width), "grp", split_axis=0, concat_axis=0, tiled=True
    )
    empty = jnp.zeros((cell_blocks, edge, width), jnp.float32)
    summed = empty.at[lists].add(returned.reshape(slots, edge, width))
    summed = summed.reshape(cell_blocks * edge, width)
    return summed.astype(jnp.bfloat16)


def per_device(jblocks, blk_row, blk_src, blk_slot, live_count, send_list, omega):
    blocks = jblocks.shape[0]
    chips, cap = lax.axis_size("grp") // 2, send_list.shape[-1]
    width = omega.shape[1]
    first = 2 * chips * cap
    count = omega.shape[0] // BLOCK
    listed = jnp.pad(send_list[0, 0].T, ((0, 0), (0, width - 2 * chips)))
    gathered, lists = gather(chips, omega, listed)
    x = jblocks.reshape(blocks, BLOCK // 2, 2 * BLOCK)
    parts, gram, my_at, their_at = local(first, lists, blk_row, blk_src, blk_slot, live_count, x, gathered)
    total = lax.psum(gram, ("grp", "pan"))
    z = give_back(chips, cap, count, parts, my_at, their_at)
    projected, gain = finish(total, z.reshape(count * BLOCK, width))
    return lax.cond(
        gain[0, 0] <= MOST_GAIN * width,
        lambda *given: projected,
        careful,
        jblocks, blk_row, blk_src, blk_slot, live_count, send_list, omega,
    )


def solution(mesh):
    placed = (
        P(("grp", "pan"), None),
        P(("grp", "pan")),
        P(("grp", "pan")),
        P(("grp", "pan")),
        P(("grp", "pan")),
        P("grp", "pan", None, None),
        P(("grp", "pan"), None),
    )
    return jax.shard_map(
        per_device, mesh=mesh, in_specs=placed, out_specs=P(("grp", "pan"), None), check_vma=False
    )
```

```python
import functools

import jax
import jax.numpy as jnp
from jax import lax
from jax.experimental import pallas as pl
from jax.experimental.pallas import tpu as pltpu
from jax.sharding import PartitionSpec as P

BLOCK = 64
RB_DEV = 4
PIECES = 2
SOME = 8
MOST_GAIN = 8.0
MESH = pl.DeviceIdType.MESH
HIGHEST = lax.Precision.HIGHEST


def places(chips):
    g = lax.axis_index("grp")
    core = lax.rem(g, 2)
    z = (g - core) // 2
    up = lax.rem(z + 1, chips) * 2 + core
    down = lax.rem(z + chips - 1, chips) * 2 + core
    return g, core, z, up, down, g + 1 - 2 * core


def greet(others):
    barrier = pltpu.get_barrier_semaphore()
    for other in others:
        pl.semaphore_signal(barrier, inc=1, device_id={"grp": other}, device_id_type=MESH)
    pl.semaphore_wait(barrier, len(others))


def gather_kernel(
    chips, mine, listed, gathered, lists, keep, ring_send, ring_recv, side_send, side_recv, own_send, own_recv,
    list_send, list_recv, list_side_send, list_side_recv,
):
    g, core, z, up, down, side = places(chips)
    half = chips // 2
    step = mine.shape[0] // PIECES

    def rows(piece):
        return pl.ds(piece * step, step)

    def owner(way, hop):
        where = z + chips - hop if way == 0 else z + hop
        return lax.rem(where, chips) * 2 + core

    def ring(way, hop, piece, from_mine=False):
        at = owner(way, hop - 1)
        source = mine.at[rows(piece)] if from_mine else gathered.at[at, rows(piece)]
        return pltpu.make_async_remote_copy(
            src_ref=source,
            dst_ref=gathered.at[at, rows(piece)],
            send_sem=ring_send.at[way, hop - 1, piece],
            recv_sem=ring_recv.at[way, hop - 1, piece],
            device_id={"grp": up if way == 0 else down},
            device_id_type=MESH,
        )

    def arrival(way, hop, piece):
        at = owner(way, hop)
        return pltpu.make_async_remote_copy(
            src_ref=gathered.at[at, rows(piece)],
            dst_ref=gathered.at[at, rows(piece)],
            send_sem=ring_send.at[way, hop - 1, piece],
            recv_sem=ring_recv.at[way, hop - 1, piece],
            device_id={"grp": up if way == 0 else down},
            device_id_type=MESH,
        )

    def across(way, hop, piece, arriving=False):
        at = owner(way, hop) + (1 - 2 * core if arriving else 0)
        return pltpu.make_async_remote_copy(
            src_ref=gathered.at[at, rows(piece)],
            dst_ref=gathered.at[at, rows(piece)],
            send_sem=side_send.at[way, hop - 1, piece],
            recv_sem=side_recv.at[way, hop - 1, piece],
            device_id={"grp": side},
            device_id_type=MESH,
        )

    def own(piece, at):
        return pltpu.make_async_remote_copy(
            src_ref=mine.at[rows(piece)],
            dst_ref=gathered.at[at, rows(piece)],
            send_sem=own_send.at[piece],
            recv_sem=own_recv.at[piece],
            device_id={"grp": side},
            device_id_type=MESH,
        )

    def last(way):
        return range(PIECES // 2) if way == 0 else range(PIECES // 2, PIECES)

    def list_ring(way, hop):
        at = owner(way, hop - 1)
        return pltpu.make_async_remote_copy(
            src_ref=lists.at[at],
            dst_ref=lists.at[at],
            send_sem=list_send.at[way, hop - 1],
            recv_sem=list_recv.at[way, hop - 1],
            device_id={"grp": up if way == 0 else down},
            device_id_type=MESH,
        )

    def list_arrival(way, hop):
        at = owner(way, hop)
        return pltpu.make_async_remote_copy(
            src_ref=lists.at[at],
            dst_ref=lists.at[at],
            send_sem=list_send.at[way, hop - 1],
            recv_sem=list_recv.at[way, hop - 1],
            device_id={"grp": up if way == 0 else down},
            device_id_type=MESH,
        )

    def list_across(way, hop, arriving=False):
        at = owner(way, hop) + (1 - 2 * core if arriving else 0)
        return pltpu.make_async_remote_copy(
            src_ref=lists.at[at],
            dst_ref=lists.at[at],
            send_sem=list_side_send.at[way, hop],
            recv_sem=list_side_recv.at[way, hop],
            device_id={"grp": side},
            device_id_type=MESH,
        )

    greet((up, down, side))
    kept = pltpu.make_async_copy(mine, gathered.at[g], keep.at[0])
    kept.start()
    listing = pltpu.make_async_copy(listed, lists.at[g], keep.at[1])
    listing.start()
    listing.wait()
    list_ring(0, 1).start()
    list_ring(1, 1).start()
    list_across(0, 0).start()
    for piece in range(PIECES):
        for way in range(2):
            ring(way, 1, piece, True).start()
    for piece in range(PIECES):
        own(piece, g).start()

    def pass_on(hop, carry):
        for way in range(2):
            list_arrival(way, hop).wait_recv()
            list_ring(way, hop + 1).start()
            list_across(way, hop).start()
        for piece in range(PIECES):
            for way in range(2):
                arrival(way, hop, piece).wait_recv()
                ring(way, hop + 1, piece).start()
                across(way, hop, piece).start()
        return carry

    lax.fori_loop(1, half - 1, pass_on, 0)
    for way in range(2):
        list_arrival(way, half - 1).wait_recv()
        list_across(way, half - 1).start()
    list_ring(0, half).start()
    list_arrival(0, half).wait_recv()
    list_across(0, half).start()
    for piece in range(PIECES):
        for way in range(2):
            arrival(way, half - 1, piece).wait_recv()
            if piece in last(way):
                ring(way, half, piece).start()
            across(way, half - 1, piece).start()
    for way in range(2):
        for piece in last(way):
            arrival(way, half, piece).wait_recv()
            across(way, half, piece).start()

    for piece in range(PIECES):
        ring(0, 1, piece, True).wait_send()
        ring(1, 1, piece, True).wait_send()
        own(piece, g).wait_send()
        own(piece, side).wait_recv()

    list_across(0, 0).wait_send()
    list_across(0, 0, True).wait_recv()
    list_ring(0, half).wait_send()
    list_across(0, half).wait_send()
    list_across(0, half, True).wait_recv()

    def finish_lists(hop, carry):
        for way in range(2):
            list_ring(way, hop).wait_send()
            list_across(way, hop).wait_send()
            list_across(way, hop, True).wait_recv()
        return carry

    lax.fori_loop(1, half, finish_lists, 0)

    def finish(hop, carry):
        for piece in range(PIECES):
            for way in range(2):
                ring(way, hop + 1, piece).wait_send()
                across(way, hop, piece).wait_send()
                across(way, hop, piece, True).wait_recv()
        return carry

    lax.fori_loop(1, half - 1, finish, 0)
    for piece in range(PIECES):
        for way in range(2):
            if piece in last(way):
                ring(way, half, piece).wait_send()
            across(way, half - 1, piece).wait_send()
            across(way, half - 1, piece, True).wait_recv()
    for way in range(2):
        for piece in last(way):
            across(way, half, piece).wait_send()
            across(way, half, piece, True).wait_recv()
    kept.wait()


def gather(chips, omega, listed):
    rows, width = omega.shape
    half = chips // 2
    dma = pltpu.SemaphoreType.DMA
    hbm = pl.BlockSpec(memory_space=pl.ANY)
    return pl.pallas_call(
        functools.partial(gather_kernel, chips),
        out_shape=[
            jax.ShapeDtypeStruct((2 * chips, rows, width), omega.dtype),
            jax.ShapeDtypeStruct((2 * chips,) + listed.shape, listed.dtype),
        ],
        in_specs=[hbm, hbm],
        out_specs=[hbm, hbm],
        scratch_shapes=[dma((2,))]
        + [dma((2, half, PIECES))] * 4
        + [dma((PIECES,))] * 2
        + [dma((2, half))] * 2
        + [dma((2, half + 1))] * 2,
        compiler_params=pltpu.CompilerParams(collective_id=0, has_side_effects=True),
    )(omega, listed)


def local_kernel(
    first, lists, blk_row, blk_src, blk_slot, live, x, cells, parts, gram, my_at, their_at, sketch, halves
):
    lane = lax.broadcasted_iota(jnp.int32, (1, 2 * BLOCK), 1)
    blocks = x.shape[0]
    owners, cap = lists.shape[0], lists.shape[1]
    g = lax.axis_index("grp")
    core = lax.rem(g, 2)
    here = lax.broadcasted_iota(jnp.int32, (1, my_at.shape[1]), 1)

    def row_of(at):
        return jnp.where(at < live[0], blk_row[at], -1)

    def slot_of(at):
        return blk_src[at] * cap + blk_slot[at]

    def place(owner, carry):
        mine = jnp.full(here.shape, owners * cap, jnp.int32)
        theirs = jnp.full(here.shape, cap, jnp.int32)
        for n in range(cap):
            mine = jnp.where(here == lists[owner, n, g], owner * cap + n, mine)
            theirs = jnp.where(here == lists[owner, n, g + 1 - 2 * core], n, theirs)
        my_at[pl.ds(owner, 1), :] = mine
        their_at[pl.ds(owner, 1), :] = theirs
        return carry

    lax.fori_loop(0, owners, place, 0)

    def pair_of(at):
        a, b = x[at], x[at + 1]
        even = jnp.concatenate([a[:, :BLOCK], b[:, :BLOCK]], axis=1)
        odd = jnp.concatenate([a[:, BLOCK:], b[:, BLOCK:]], axis=1)
        both = jnp.concatenate([even, odd], axis=0)
        rows = jnp.where(lane < BLOCK, row_of(at), row_of(at + 1))
        return jnp.concatenate(
            [both * jnp.where(rows == r, 1.0, 0.0).astype(both.dtype) for r in range(RB_DEV)], axis=0
        )

    def some_of(at):
        return jnp.concatenate([pair_of(at + n) for n in range(0, SOME, 2)], axis=1)

    def cell_rows(at):
        first_row = lists[blk_src[at], blk_slot[at], g] * BLOCK
        return cells[blk_src[at], pl.ds(pl.multiple_of(first_row, BLOCK), BLOCK), :]

    sketch[...] = jnp.zeros_like(sketch)

    def forward(i, carry):
        at = i * SOME
        picked = jnp.concatenate([cell_rows(at + n) for n in range(SOME)], axis=0)
        sketch[...] += jnp.dot(some_of(at), picked, preferred_element_type=jnp.float32)
        return carry

    lax.fori_loop(0, blocks // SOME, forward, 0, unroll=2)
    s = sketch[...]
    gram[...] = lax.dot_general(
        s, s, (((0,), (0,)), ((), ())), precision=HIGHEST, preferred_element_type=jnp.float32
    )
    high = s.astype(jnp.bfloat16)
    low = (s - high.astype(jnp.float32)).astype(jnp.bfloat16)
    halves[...] = jnp.concatenate([high, low], axis=1)
    width = s.shape[1]

    def back(at):
        two = lax.dot_general(
            some_of(at), halves[...], (((0,), (0,)), ((), ())), preferred_element_type=jnp.float32
        )
        return two[:, :width] + two[:, width:]

    def base(i, carry):
        made = back(i * SOME)
        for n in range(SOME):
            parts[i * SOME + n] = made[n * BLOCK : (n + 1) * BLOCK]
        return carry

    lax.fori_loop(0, first // SOME, base, 0, unroll=2)
    parts[first] = jnp.zeros((BLOCK, width), jnp.float32)

    def extra(i, carry):
        made = back(i * SOME)
        for n in range(SOME):
            parts[slot_of(i * SOME + n)] += made[n * BLOCK : (n + 1) * BLOCK]
        return carry

    lax.fori_loop(first // SOME, blocks // SOME, extra, 0)


def local(first, lists, blk_row, blk_src, blk_slot, live, x, cells):
    width = cells.shape[-1]
    owners = cells.shape[0]
    smem = pl.BlockSpec(memory_space=pltpu.SMEM)
    vmem = pl.BlockSpec(memory_space=pltpu.VMEM)
    return pl.pallas_call(
        functools.partial(local_kernel, first),
        out_shape=[
            jax.ShapeDtypeStruct((first + 1, BLOCK, width), jnp.float32),
            jax.ShapeDtypeStruct((width, width), jnp.float32),
            jax.ShapeDtypeStruct((owners, width), jnp.int32),
            jax.ShapeDtypeStruct((owners, width), jnp.int32),
        ],
        in_specs=[smem, smem, smem, smem, smem, vmem, vmem],
        out_specs=[vmem] * 4,
        scratch_shapes=[
            pltpu.VMEM((RB_DEV * BLOCK, width), jnp.float32),
            pltpu.VMEM((RB_DEV * BLOCK, 2 * width), jnp.bfloat16),
        ],
        compiler_params=pltpu.CompilerParams(vmem_limit_bytes=56 * 1024 * 1024),
    )(lists, blk_row, blk_src, blk_slot, live, x, cells)


def flip(index, step):
    return index + step - 2 * step * lax.rem(index // step, 2)


def sum_kernel(axis, rounds, value, total, held, got, send, recv):
    at = lax.axis_index(axis)
    barrier = pltpu.get_barrier_semaphore()
    for i in range(rounds):
        pl.semaphore_signal(barrier, inc=1, device_id={axis: flip(at, 1 << i)}, device_id_type=MESH)
    pl.semaphore_wait(barrier, rounds)
    held[0] = value[...]
    copies = []
    for i in range(rounds):
        copy = pltpu.make_async_remote_copy(
            src_ref=held.at[i], dst_ref=got.at[i], send_sem=send.at[i], recv_sem=recv.at[i],
            device_id={axis: flip(at, 1 << i)}, device_id_type=MESH,
        )
        copy.start()
        copy.wait_recv()
        held[i + 1] = held[i] + got[i]
        copies.append(copy)
    total[...] = held[rounds]
    for copy in copies:
        copy.wait_send()


def sum_over(axis, size, value):
    rounds = size.bit_length() - 1
    if rounds == 0:
        return value
    vmem = pl.BlockSpec(memory_space=pltpu.VMEM)
    return pl.pallas_call(
        functools.partial(sum_kernel, axis, rounds),
        out_shape=jax.ShapeDtypeStruct(value.shape, value.dtype),
        in_specs=[vmem],
        out_specs=vmem,
        scratch_shapes=[
            pltpu.VMEM((rounds + 1,) + value.shape, value.dtype),
            pltpu.VMEM((rounds,) + value.shape, value.dtype),
            pltpu.SemaphoreType.DMA((rounds,)),
            pltpu.SemaphoreType.DMA((rounds,)),
        ],
        compiler_params=pltpu.CompilerParams(collective_id=2, has_side_effects=True),
    )(value)


def return_kernel(
    chips, cap, rounds, parts, gram, mine, theirs, out, gain,
    other_far, other_next, other, sent, got, sent_scale, got_scale, grams, grams_got, a, v, factors, z_buf,
    side_send, side_recv, ring_send, ring_recv, scale_send, scale_recv, gram_send, gram_recv,
):
    g, core, z, up, down, side = places(chips)
    half = chips // 2
    width = out.shape[1]
    count = out.shape[0] // BLOCK
    size = count // PIECES
    met = [flip(g, 1 << i) for i in range(rounds)]
    greet([up, down, side] + met)

    def gram_copy(i):
        return pltpu.make_async_remote_copy(
            src_ref=grams.at[i], dst_ref=grams_got.at[i], send_sem=gram_send.at[i], recv_sem=gram_recv.at[i],
            device_id={"grp": met[i]}, device_id_type=MESH,
        )

    def gram_round(i):
        gram_copy(i).wait_recv()
        grams[i + 1] = grams[i] + grams_got[i]
        if i + 1 < rounds:
            gram_copy(i + 1).start()

    def chip(n):
        return lax.rem(z + n, chips)

    def across(n, to):
        at = chip(n)
        return pltpu.make_async_remote_copy(
            src_ref=parts.at[pl.ds((at * 2 + 1 - core) * cap, cap)],
            dst_ref=to.at[pl.ds(0, cap)],
            send_sem=side_send.at[n],
            recv_sem=side_recv.at[n],
            device_id={"grp": side},
            device_id_type=MESH,
        )

    early = [(half, other_far.at[0]), (half - 1, other_next.at[0]), (half + 1, other_next.at[1])]

    def rest(act):
        def one(n, carry):
            act(across(n, other.at[n]))
            return carry

        lax.fori_loop(0, half - 1, one, 0)
        lax.fori_loop(half + 2, chips, one, 0)

    def blocks(piece):
        return pl.ds(piece * size, size)

    def ring(way, hop, piece):
        to = {"grp": up if way == 0 else down}
        values = pltpu.make_async_remote_copy(
            src_ref=sent.at[way, hop, blocks(piece)],
            dst_ref=got.at[way, hop, blocks(piece)],
            send_sem=ring_send.at[way, hop, piece],
            recv_sem=ring_recv.at[way, hop, piece],
            device_id=to,
            device_id_type=MESH,
        )
        scales = pltpu.make_async_remote_copy(
            src_ref=sent_scale.at[way, hop, blocks(piece)],
            dst_ref=got_scale.at[way, hop, blocks(piece)],
            send_sem=scale_send.at[way, hop, piece],
            recv_sem=scale_recv.at[way, hop, piece],
            device_id=to,
            device_id_type=MESH,
        )
        return values, scales

    for n, to in early:
        across(n, to).start()
    rest(lambda copy: copy.start())
    grams[0] = gram[...]
    gram_copy(0).start()
    nothing = jnp.zeros((BLOCK, width), jnp.float32)
    other_far[0, cap] = nothing
    for n in range(2):
        other_next[n, cap] = nothing
    for n in range(chips):
        other[n, cap] = nothing

    def own(n, q, held=None, line=0):
        owner = chip(n) * 2 + core
        if held is None:
            return parts[mine[owner, q]] + other[n, theirs[owner, q]]
        return parts[mine[owner, q]] + held[line, theirs[owner, q]]

    def read(way, hop, q):
        return got[way, hop, q].astype(jnp.int32).astype(jnp.float32) * got_scale[way, hop, pl.ds(q, 1), :]

    def await_piece(way, hop, piece):
        for copy in ring(way, hop, piece):
            copy.wait_recv()

    def send(way, hop, piece, onward, held=None):
        n = half - hop if way == 0 else half + hop
        if onward:
            await_piece(way, hop - 1, piece)

        def block(q, carry):
            total = own(n, q, held, way if held is other_next else 0)
            if onward:
                total = total + read(way, hop - 1, q)
            top = jnp.max(jnp.abs(total), axis=0, keepdims=True)
            usable = top > 1e-30
            factor = jnp.where(usable, 32767.0 / jnp.where(usable, top, 1.0), 0.0)
            sent[way, hop, q] = jnp.round(total * factor).astype(jnp.int32).astype(jnp.int16)
            sent_scale[way, hop, pl.ds(q, 1), :] = top * (1.0 / 32767.0)
            return carry

        lax.fori_loop(piece * size, (piece + 1) * size, block, 0)
        for copy in ring(way, hop, piece):
            copy.start()

    def first(way):
        return range(PIECES // 2) if way == 0 else range(PIECES // 2, PIECES)

    wide = lax.broadcasted_iota(jnp.int32, (width, width), 1)
    tall = lax.broadcasted_iota(jnp.int32, (width, width), 0)

    def pivot(j, carry):
        old = a[...]
        row_a, row_v = a[pl.ds(j, 1), :], v[pl.ds(j, 1), :]
        d = jnp.sum(jnp.where(wide[:1] == j, row_a, 0.0), axis=1, keepdims=True)
        column = jnp.sum(jnp.where(wide == j, old, 0.0), axis=1, keepdims=True)
        factor = jnp.where(tall > j, column / d, 0.0)
        a[...] = old - factor * row_a
        v[...] = v[...] - factor * row_v
        return carry

    across(*early[0]).wait_recv()
    for way in range(2):
        for piece in first(way):
            send(way, 0, piece, False, other_far)
    gram_round(0)
    for n, to in early[1:]:
        across(n, to).wait_recv()
    turn = 1
    for piece in range(PIECES):
        for way in range(2):
            at = PIECES - 1 - piece if way == 0 else piece
            send(way, 1, at, at in first(way), other_next)
            if turn < rounds:
                gram_round(turn)
                turn += 1
    while turn < rounds:
        gram_round(turn)
        turn += 1
    a[...] = grams[rounds]
    v[...] = jnp.where(wide == tall, 1.0, 0.0)
    rest(lambda copy: copy.wait_recv())
    points = (half - 2) * PIECES * 2
    each = width // points
    lead = width - each * points
    lax.fori_loop(0, lead, pivot, 0)

    def onward(hop, carry):
        for piece in range(PIECES):
            for way in range(2):
                send(way, hop, PIECES - 1 - piece if way == 0 else piece, True)
                start = lead + (((hop - 2) * PIECES + piece) * 2 + way) * each
                lax.fori_loop(start, start + each, pivot, 0)
        return carry

    lax.fori_loop(2, half, onward, 0)

    d = jnp.sum(jnp.where(wide == tall, a[...], 0.0), axis=1, keepdims=True)
    inverse = v[...] / jnp.sqrt(d)
    spread = jnp.sum(jnp.where(wide == tall, grams[rounds], 0.0), axis=0, keepdims=True)
    grown = jnp.sum(inverse * inverse * spread, axis=1, keepdims=True)
    gain[...] = jnp.broadcast_to(jnp.sum(grown, axis=0, keepdims=True), gain.shape)
    high = inverse.astype(jnp.bfloat16)
    low = (inverse - high.astype(jnp.float32)).astype(jnp.bfloat16)
    factors[...] = jnp.concatenate(
        [
            jnp.concatenate([high, high], axis=1),
            jnp.concatenate([low, jnp.zeros_like(low)], axis=1),
        ],
        axis=0,
    )

    for piece in range(PIECES):
        for way in range(2):
            await_piece(way, half - 1, piece)

        def block(q, carry):
            z_buf[pl.ds(pl.multiple_of(q * BLOCK, BLOCK), BLOCK), :] = (
                own(0, q) + read(0, half - 1, q) + read(1, half - 1, q)
            )
            return carry

        lax.fori_loop(piece * size, (piece + 1) * size, block, 0)

        def product(i, carry):
            at = pl.ds(pl.multiple_of(i * 256, 256), 256)
            value = z_buf[at, :]
            top = value.astype(jnp.bfloat16)
            left = (value - top.astype(jnp.float32)).astype(jnp.bfloat16)
            two = lax.dot_general(
                jnp.concatenate([top, left], axis=1), factors[...], (((1,), (1,)), ((), ())),
                preferred_element_type=jnp.float32,
            )
            out[at, :] = (two[:, :width] + two[:, width:]).astype(out.dtype)
            return carry

        per = size * BLOCK // 256
        lax.fori_loop(piece * per, (piece + 1) * per, product, 0)

    def finish(way, hop, piece):
        for copy in ring(way, hop, piece):
            copy.wait_send()

    for way in range(2):
        for piece in first(way):
            finish(way, 0, piece)

    def finish_all(hop, carry):
        for piece in range(PIECES):
            for way in range(2):
                finish(way, hop, piece)
        return carry

    lax.fori_loop(1, half, finish_all, 0)
    for n, to in early:
        across(n, to).wait_send()
    rest(lambda copy: copy.wait_send())
    for i in range(rounds):
        gram_copy(i).wait_send()


def give_back(chips, cap, count, parts, gram, mine, theirs):
    edge, width = parts.shape[1:]
    half = chips // 2
    rounds = (2 * chips).bit_length() - 1
    dma = pltpu.SemaphoreType.DMA
    smem = pl.BlockSpec(memory_space=pltpu.SMEM)
    vmem = pl.BlockSpec(memory_space=pltpu.VMEM)
    f32 = jnp.float32
    return pl.pallas_call(
        functools.partial(return_kernel, chips, cap, rounds),
        out_shape=[
            jax.ShapeDtypeStruct((count * edge, width), jnp.bfloat16),
            jax.ShapeDtypeStruct((8, width), f32),
        ],
        in_specs=[vmem, vmem, smem, smem],
        out_specs=[vmem, vmem],
        scratch_shapes=[
            pltpu.VMEM((1, cap + 1, edge, width), f32),
            pltpu.VMEM((2, cap + 1, edge, width), f32),
            pltpu.VMEM((chips, cap + 1, edge, width), f32),
            pltpu.VMEM((2, half, count, edge, width), jnp.int16),
            pltpu.VMEM((2, half, count, edge, width), jnp.int16),
            pltpu.VMEM((2, half, count, width), f32),
            pltpu.VMEM((2, half, count, width), f32),
            pltpu.VMEM((rounds + 1, width, width), f32),
            pltpu.VMEM((rounds, width, width), f32),
            pltpu.VMEM((width, width), f32),
            pltpu.VMEM((width, width), f32),
            pltpu.VMEM((2 * width, 2 * width), jnp.bfloat16),
            pltpu.VMEM((count * edge, width), f32),
            dma((chips,)),
            dma((chips,)),
            dma((2, half, PIECES)),
            dma((2, half, PIECES)),
            dma((2, half, PIECES)),
            dma((2, half, PIECES)),
            dma((rounds,)),
            dma((rounds,)),
        ],
        compiler_params=pltpu.CompilerParams(
            collective_id=1, has_side_effects=True, vmem_limit_bytes=56 * 1024 * 1024
        ),
    )(parts, gram, mine, theirs)


def factor_of(sketch):
    local_gram = jnp.dot(sketch.T, sketch, precision=lax.Precision.HIGHEST)
    gram = lax.psum(local_gram, ("grp", "pan"))
    return jnp.linalg.cholesky(gram)


def careful(jblocks, blk_row, blk_src, blk_slot, live_count, send_list, omega):
    block_count = jblocks.shape[0]
    width = omega.shape[1]
    groups = lax.axis_size("grp")
    lists = send_list.reshape(-1)
    slots = lists.shape[0]
    cap = slots // groups
    edge = BLOCK
    cell_blocks = omega.shape[0] // edge
    alive = jnp.arange(block_count, dtype=jnp.int32) < live_count[0]
    values = jnp.where(alive[:, None], jblocks, jnp.zeros((), jblocks.dtype)).reshape(
        block_count, edge, edge
    )
    omega_blocks = omega.reshape(cell_blocks, edge, width)
    outgoing = jnp.take(omega_blocks, lists, axis=0).reshape(groups, cap * edge, width)
    incoming = lax.all_to_all(outgoing, "grp", split_axis=0, concat_axis=0, tiled=True).reshape(
        slots, edge, width
    )
    slot_index = blk_src * cap + blk_slot
    picked = jnp.take(incoming, slot_index, axis=0)
    products = jnp.einsum("bij,bjk->bik", values, picked, preferred_element_type=jnp.float32)
    sketch = jax.ops.segment_sum(products, blk_row, num_segments=RB_DEV)
    sketch = sketch.reshape(RB_DEV * edge, width)
    lower = factor_of(sketch)
    used_rows = lax.linalg.triangular_solve(lower, sketch.T, left_side=True, lower=True).T
    chosen = jnp.take(used_rows.reshape(RB_DEV, edge, width), blk_row, axis=0)
    terms = jnp.einsum(
        "bij,bik->bjk",
        values.astype(jnp.float32),
        chosen,
        precision=lax.Precision.HIGH,
        preferred_element_type=jnp.float32,
    )
    per_slot = terms[:slots].at[slot_index[slots:]].add(terms[slots:])
    returned = lax.all_to_all(
        per_slot.reshape(groups, cap * edge, width), "grp", split_axis=0, concat_axis=0, tiled=True
    )
    empty = jnp.zeros((cell_blocks, edge, width), jnp.float32)
    summed = empty.at[lists].add(returned.reshape(slots, edge, width))
    summed = summed.reshape(cell_blocks * edge, width)
    return summed.astype(jnp.bfloat16)


def per_device(jblocks, blk_row, blk_src, blk_slot, live_count, send_list, omega):
    blocks = jblocks.shape[0]
    chips, cap = lax.axis_size("grp") // 2, send_list.shape[-1]
    width = omega.shape[1]
    first = 2 * chips * cap
    count = omega.shape[0] // BLOCK
    listed = jnp.pad(send_list[0, 0].T, ((0, 0), (0, width - 2 * chips)))
    gathered, lists = gather(chips, omega, listed)
    x = jblocks.reshape(blocks, BLOCK // 2, 2 * BLOCK)
    parts, gram, my_at, their_at = local(first, lists, blk_row, blk_src, blk_slot, live_count, x, gathered)
    gram = sum_over("pan", lax.axis_size("pan"), gram)
    projected, gain = give_back(chips, cap, count, parts, gram, my_at, their_at)
    return lax.cond(
        gain[0, 0] <= MOST_GAIN * width,
        lambda *given: projected,
        careful,
        jblocks, blk_row, blk_src, blk_slot, live_count, send_list, omega,
    )


def solution(mesh):
    placed = (
        P(("grp", "pan"), None),
        P(("grp", "pan")),
        P(("grp", "pan")),
        P(("grp", "pan")),
        P(("grp", "pan")),
        P("grp", "pan", None, None),
        P(("grp", "pan"), None),
    )
    return jax.shard_map(
        per_device, mesh=mesh, in_specs=placed, out_specs=P(("grp", "pan"), None), check_vma=False
    )
```

```python
import functools

import jax
import jax.numpy as jnp
from jax import lax
from jax.experimental import pallas as pl
from jax.experimental.pallas import tpu as pltpu
from jax.sharding import PartitionSpec as P

BLOCK = 64
RB_DEV = 4
PIECES = 2
SOME = 8
GROUP = 4
MOST_GAIN = 8.0
MESH = pl.DeviceIdType.MESH
HIGHEST = lax.Precision.HIGHEST


def places(chips):
    g = lax.axis_index("grp")
    core = lax.rem(g, 2)
    z = (g - core) // 2
    up = lax.rem(z + 1, chips) * 2 + core
    down = lax.rem(z + chips - 1, chips) * 2 + core
    return g, core, z, up, down, g + 1 - 2 * core


def greet(others):
    barrier = pltpu.get_barrier_semaphore()
    for other in others:
        pl.semaphore_signal(barrier, inc=1, device_id={"grp": other}, device_id_type=MESH)
    pl.semaphore_wait(barrier, len(others))


def gather_kernel(
    chips, mine, listed, gathered, lists, keep, ring_send, ring_recv, side_send, side_recv, own_send, own_recv,
    list_send, list_recv, list_side_send, list_side_recv,
):
    g, core, z, up, down, side = places(chips)
    half = chips // 2
    step = mine.shape[0] // PIECES

    def rows(piece):
        return pl.ds(piece * step, step)

    def owner(way, hop):
        where = z + chips - hop if way == 0 else z + hop
        return lax.rem(where, chips) * 2 + core

    def ring(way, hop, piece, from_mine=False):
        at = owner(way, hop - 1)
        source = mine.at[rows(piece)] if from_mine else gathered.at[at, rows(piece)]
        return pltpu.make_async_remote_copy(
            src_ref=source,
            dst_ref=gathered.at[at, rows(piece)],
            send_sem=ring_send.at[way, hop - 1, piece],
            recv_sem=ring_recv.at[way, hop - 1, piece],
            device_id={"grp": up if way == 0 else down},
            device_id_type=MESH,
        )

    def arrival(way, hop, piece):
        at = owner(way, hop)
        return pltpu.make_async_remote_copy(
            src_ref=gathered.at[at, rows(piece)],
            dst_ref=gathered.at[at, rows(piece)],
            send_sem=ring_send.at[way, hop - 1, piece],
            recv_sem=ring_recv.at[way, hop - 1, piece],
            device_id={"grp": up if way == 0 else down},
            device_id_type=MESH,
        )

    def across(way, hop, piece, arriving=False):
        at = owner(way, hop) + (1 - 2 * core if arriving else 0)
        return pltpu.make_async_remote_copy(
            src_ref=gathered.at[at, rows(piece)],
            dst_ref=gathered.at[at, rows(piece)],
            send_sem=side_send.at[way, hop - 1, piece],
            recv_sem=side_recv.at[way, hop - 1, piece],
            device_id={"grp": side},
            device_id_type=MESH,
        )

    def own(piece, at):
        return pltpu.make_async_remote_copy(
            src_ref=mine.at[rows(piece)],
            dst_ref=gathered.at[at, rows(piece)],
            send_sem=own_send.at[piece],
            recv_sem=own_recv.at[piece],
            device_id={"grp": side},
            device_id_type=MESH,
        )

    def last(way):
        return range(PIECES // 2) if way == 0 else range(PIECES // 2, PIECES)

    def list_ring(way, hop):
        at = owner(way, hop - 1)
        return pltpu.make_async_remote_copy(
            src_ref=lists.at[at],
            dst_ref=lists.at[at],
            send_sem=list_send.at[way, hop - 1],
            recv_sem=list_recv.at[way, hop - 1],
            device_id={"grp": up if way == 0 else down},
            device_id_type=MESH,
        )

    def list_arrival(way, hop):
        at = owner(way, hop)
        return pltpu.make_async_remote_copy(
            src_ref=lists.at[at],
            dst_ref=lists.at[at],
            send_sem=list_send.at[way, hop - 1],
            recv_sem=list_recv.at[way, hop - 1],
            device_id={"grp": up if way == 0 else down},
            device_id_type=MESH,
        )

    def list_across(way, hop, arriving=False):
        at = owner(way, hop) + (1 - 2 * core if arriving else 0)
        return pltpu.make_async_remote_copy(
            src_ref=lists.at[at],
            dst_ref=lists.at[at],
            send_sem=list_side_send.at[way, hop],
            recv_sem=list_side_recv.at[way, hop],
            device_id={"grp": side},
            device_id_type=MESH,
        )

    greet((up, down, side))
    kept = pltpu.make_async_copy(mine, gathered.at[g], keep.at[0])
    kept.start()
    listing = pltpu.make_async_copy(listed, lists.at[g], keep.at[1])
    listing.start()
    listing.wait()
    list_ring(0, 1).start()
    list_ring(1, 1).start()
    list_across(0, 0).start()
    for piece in range(PIECES):
        for way in range(2):
            ring(way, 1, piece, True).start()
    for piece in range(PIECES):
        own(piece, g).start()

    def pass_on(hop, carry):
        for way in range(2):
            list_arrival(way, hop).wait_recv()
            list_ring(way, hop + 1).start()
            list_across(way, hop).start()
        for piece in range(PIECES):
            for way in range(2):
                arrival(way, hop, piece).wait_recv()
                ring(way, hop + 1, piece).start()
                across(way, hop, piece).start()
        return carry

    lax.fori_loop(1, half - 1, pass_on, 0)
    for way in range(2):
        list_arrival(way, half - 1).wait_recv()
        list_across(way, half - 1).start()
    list_ring(0, half).start()
    list_arrival(0, half).wait_recv()
    list_across(0, half).start()
    for piece in range(PIECES):
        for way in range(2):
            arrival(way, half - 1, piece).wait_recv()
            if piece in last(way):
                ring(way, half, piece).start()
            across(way, half - 1, piece).start()
    for way in range(2):
        for piece in last(way):
            arrival(way, half, piece).wait_recv()
            across(way, half, piece).start()

    for piece in range(PIECES):
        ring(0, 1, piece, True).wait_send()
        ring(1, 1, piece, True).wait_send()
        own(piece, g).wait_send()
        own(piece, side).wait_recv()

    list_across(0, 0).wait_send()
    list_across(0, 0, True).wait_recv()
    list_ring(0, half).wait_send()
    list_across(0, half).wait_send()
    list_across(0, half, True).wait_recv()

    def finish_lists(hop, carry):
        for way in range(2):
            list_ring(way, hop).wait_send()
            list_across(way, hop).wait_send()
            list_across(way, hop, True).wait_recv()
        return carry

    lax.fori_loop(1, half, finish_lists, 0)

    def finish(hop, carry):
        for piece in range(PIECES):
            for way in range(2):
                ring(way, hop + 1, piece).wait_send()
                across(way, hop, piece).wait_send()
                across(way, hop, piece, True).wait_recv()
        return carry

    lax.fori_loop(1, half - 1, finish, 0)
    for piece in range(PIECES):
        for way in range(2):
            if piece in last(way):
                ring(way, half, piece).wait_send()
            across(way, half - 1, piece).wait_send()
            across(way, half - 1, piece, True).wait_recv()
    for way in range(2):
        for piece in last(way):
            across(way, half, piece).wait_send()
            across(way, half, piece, True).wait_recv()
    kept.wait()


def gather(chips, omega, listed):
    rows, width = omega.shape
    half = chips // 2
    dma = pltpu.SemaphoreType.DMA
    hbm = pl.BlockSpec(memory_space=pl.ANY)
    return pl.pallas_call(
        functools.partial(gather_kernel, chips),
        out_shape=[
            jax.ShapeDtypeStruct((2 * chips, rows, width), omega.dtype),
            jax.ShapeDtypeStruct((2 * chips,) + listed.shape, listed.dtype),
        ],
        in_specs=[hbm, hbm],
        out_specs=[hbm, hbm],
        scratch_shapes=[dma((2,))]
        + [dma((2, half, PIECES))] * 4
        + [dma((PIECES,))] * 2
        + [dma((2, half))] * 2
        + [dma((2, half + 1))] * 2,
        compiler_params=pltpu.CompilerParams(collective_id=0, has_side_effects=True),
    )(omega, listed)


def local_kernel(
    first, lists, blk_row, blk_src, blk_slot, live, x, cells, parts, gram, my_at, their_at, sketch, halves
):
    lane = lax.broadcasted_iota(jnp.int32, (1, 2 * BLOCK), 1)
    blocks = x.shape[0]
    owners, cap = lists.shape[0], lists.shape[1]
    g = lax.axis_index("grp")
    core = lax.rem(g, 2)
    here = lax.broadcasted_iota(jnp.int32, (1, my_at.shape[1]), 1)

    def row_of(at):
        return jnp.where(at < live[0], blk_row[at], -1)

    def slot_of(at):
        return blk_src[at] * cap + blk_slot[at]

    def place(owner, carry):
        mine = jnp.full(here.shape, owners * cap, jnp.int32)
        theirs = jnp.full(here.shape, cap, jnp.int32)
        for n in range(cap):
            mine = jnp.where(here == lists[owner, n, g], owner * cap + n, mine)
            theirs = jnp.where(here == lists[owner, n, g + 1 - 2 * core], n, theirs)
        my_at[pl.ds(owner, 1), :] = mine
        their_at[pl.ds(owner, 1), :] = theirs
        return carry

    lax.fori_loop(0, owners, place, 0)

    def pair_of(at):
        a, b = x[at], x[at + 1]
        even = jnp.concatenate([a[:, :BLOCK], b[:, :BLOCK]], axis=1)
        odd = jnp.concatenate([a[:, BLOCK:], b[:, BLOCK:]], axis=1)
        both = jnp.concatenate([even, odd], axis=0)
        rows = jnp.where(lane < BLOCK, row_of(at), row_of(at + 1))
        return jnp.concatenate(
            [both * jnp.where(rows == r, 1.0, 0.0).astype(both.dtype) for r in range(RB_DEV)], axis=0
        )

    def some_of(at):
        return jnp.concatenate([pair_of(at + n) for n in range(0, SOME, 2)], axis=1)

    def cell_rows(at):
        first_row = lists[blk_src[at], blk_slot[at], g] * BLOCK
        return cells[blk_src[at], pl.ds(pl.multiple_of(first_row, BLOCK), BLOCK), :]

    sketch[...] = jnp.zeros_like(sketch)

    def forward(i, carry):
        at = i * SOME
        picked = jnp.concatenate([cell_rows(at + n) for n in range(SOME)], axis=0)
        sketch[...] += jnp.dot(some_of(at), picked, preferred_element_type=jnp.float32)
        return carry

    lax.fori_loop(0, blocks // SOME, forward, 0, unroll=2)
    s = sketch[...]
    gram[...] = lax.dot_general(
        s, s, (((0,), (0,)), ((), ())), precision=HIGHEST, preferred_element_type=jnp.float32
    )
    high = s.astype(jnp.bfloat16)
    low = (s - high.astype(jnp.float32)).astype(jnp.bfloat16)
    halves[...] = jnp.concatenate([high, low], axis=1)
    width = s.shape[1]

    def back(at):
        two = lax.dot_general(
            some_of(at), halves[...], (((0,), (0,)), ((), ())), preferred_element_type=jnp.float32
        )
        return two[:, :width] + two[:, width:]

    def base(i, carry):
        made = back(i * SOME)
        for n in range(SOME):
            parts[i * SOME + n] = made[n * BLOCK : (n + 1) * BLOCK]
        return carry

    lax.fori_loop(0, first // SOME, base, 0, unroll=2)
    parts[first] = jnp.zeros((BLOCK, width), jnp.float32)

    def extra(i, carry):
        made = back(i * SOME)
        for n in range(SOME):
            parts[slot_of(i * SOME + n)] += made[n * BLOCK : (n + 1) * BLOCK]
        return carry

    lax.fori_loop(first // SOME, blocks // SOME, extra, 0)


def local(first, lists, blk_row, blk_src, blk_slot, live, x, cells):
    width = cells.shape[-1]
    owners = cells.shape[0]
    smem = pl.BlockSpec(memory_space=pltpu.SMEM)
    vmem = pl.BlockSpec(memory_space=pltpu.VMEM)
    return pl.pallas_call(
        functools.partial(local_kernel, first),
        out_shape=[
            jax.ShapeDtypeStruct((first + 1, BLOCK, width), jnp.float32),
            jax.ShapeDtypeStruct((width, width), jnp.float32),
            jax.ShapeDtypeStruct((owners, width), jnp.int32),
            jax.ShapeDtypeStruct((owners, width), jnp.int32),
        ],
        in_specs=[smem, smem, smem, smem, smem, vmem, vmem],
        out_specs=[vmem] * 4,
        scratch_shapes=[
            pltpu.VMEM((RB_DEV * BLOCK, width), jnp.float32),
            pltpu.VMEM((RB_DEV * BLOCK, 2 * width), jnp.bfloat16),
        ],
        compiler_params=pltpu.CompilerParams(vmem_limit_bytes=56 * 1024 * 1024),
    )(lists, blk_row, blk_src, blk_slot, live, x, cells)


def flip(index, step):
    return index + step - 2 * step * lax.rem(index // step, 2)


def sum_kernel(axis, rounds, value, total, held, got, send, recv):
    at = lax.axis_index(axis)
    barrier = pltpu.get_barrier_semaphore()
    for i in range(rounds):
        pl.semaphore_signal(barrier, inc=1, device_id={axis: flip(at, 1 << i)}, device_id_type=MESH)
    pl.semaphore_wait(barrier, rounds)
    held[0] = value[...]
    copies = []
    for i in range(rounds):
        copy = pltpu.make_async_remote_copy(
            src_ref=held.at[i], dst_ref=got.at[i], send_sem=send.at[i], recv_sem=recv.at[i],
            device_id={axis: flip(at, 1 << i)}, device_id_type=MESH,
        )
        copy.start()
        copy.wait_recv()
        held[i + 1] = held[i] + got[i]
        copies.append(copy)
    total[...] = held[rounds]
    for copy in copies:
        copy.wait_send()


def sum_over(axis, size, value):
    rounds = size.bit_length() - 1
    if rounds == 0:
        return value
    vmem = pl.BlockSpec(memory_space=pltpu.VMEM)
    return pl.pallas_call(
        functools.partial(sum_kernel, axis, rounds),
        out_shape=jax.ShapeDtypeStruct(value.shape, value.dtype),
        in_specs=[vmem],
        out_specs=vmem,
        scratch_shapes=[
            pltpu.VMEM((rounds + 1,) + value.shape, value.dtype),
            pltpu.VMEM((rounds,) + value.shape, value.dtype),
            pltpu.SemaphoreType.DMA((rounds,)),
            pltpu.SemaphoreType.DMA((rounds,)),
        ],
        compiler_params=pltpu.CompilerParams(collective_id=2, has_side_effects=True),
    )(value)


def return_kernel(
    chips, cap, rounds, parts, gram, mine, theirs, out, gain,
    other_far, other_next, other, sent, got, sent_scale, got_scale, grams, grams_got, a, v, factors, z_buf,
    side_send, side_recv, ring_send, ring_recv, scale_send, scale_recv, gram_send, gram_recv,
):
    g, core, z, up, down, side = places(chips)
    half = chips // 2
    width = out.shape[1]
    count = out.shape[0] // BLOCK
    size = count // PIECES
    met = [flip(g, 1 << i) for i in range(rounds)]
    greet([up, down, side] + met)

    def gram_copy(i):
        return pltpu.make_async_remote_copy(
            src_ref=grams.at[i], dst_ref=grams_got.at[i], send_sem=gram_send.at[i], recv_sem=gram_recv.at[i],
            device_id={"grp": met[i]}, device_id_type=MESH,
        )

    def gram_round(i):
        gram_copy(i).wait_recv()
        grams[i + 1] = grams[i] + grams_got[i]
        if i + 1 < rounds:
            gram_copy(i + 1).start()

    def chip(n):
        return lax.rem(z + n, chips)

    def across(n, to):
        at = chip(n)
        return pltpu.make_async_remote_copy(
            src_ref=parts.at[pl.ds((at * 2 + 1 - core) * cap, cap)],
            dst_ref=to.at[pl.ds(0, cap)],
            send_sem=side_send.at[n],
            recv_sem=side_recv.at[n],
            device_id={"grp": side},
            device_id_type=MESH,
        )

    early = [(half, other_far.at[0]), (half - 1, other_next.at[0]), (half + 1, other_next.at[1])]

    def rest(act):
        def one(n, carry):
            act(across(n, other.at[n]))
            return carry

        lax.fori_loop(0, half - 1, one, 0)
        lax.fori_loop(half + 2, chips, one, 0)

    def blocks(piece):
        return pl.ds(piece * size, size)

    def ring(way, hop, piece):
        to = {"grp": up if way == 0 else down}
        values = pltpu.make_async_remote_copy(
            src_ref=sent.at[way, hop, blocks(piece)],
            dst_ref=got.at[way, hop, blocks(piece)],
            send_sem=ring_send.at[way, hop, piece],
            recv_sem=ring_recv.at[way, hop, piece],
            device_id=to,
            device_id_type=MESH,
        )
        scales = pltpu.make_async_remote_copy(
            src_ref=sent_scale.at[way, hop, blocks(piece)],
            dst_ref=got_scale.at[way, hop, blocks(piece)],
            send_sem=scale_send.at[way, hop, piece],
            recv_sem=scale_recv.at[way, hop, piece],
            device_id=to,
            device_id_type=MESH,
        )
        return values, scales

    for n, to in early:
        across(n, to).start()
    rest(lambda copy: copy.start())
    grams[0] = gram[...]
    gram_copy(0).start()
    nothing = jnp.zeros((BLOCK, width), jnp.float32)
    other_far[0, cap] = nothing
    for n in range(2):
        other_next[n, cap] = nothing
    for n in range(chips):
        other[n, cap] = nothing

    def own(n, q, held=None, line=0):
        owner = chip(n) * 2 + core
        if held is None:
            return parts[mine[owner, q]] + other[n, theirs[owner, q]]
        return parts[mine[owner, q]] + held[line, theirs[owner, q]]

    def read(way, hop, q):
        return got[way, hop, q].astype(jnp.int32).astype(jnp.float32) * got_scale[way, hop, pl.ds(q, 1), :]

    def await_piece(way, hop, piece):
        for copy in ring(way, hop, piece):
            copy.wait_recv()

    def send(way, hop, piece, onward, held=None):
        n = half - hop if way == 0 else half + hop
        if onward:
            await_piece(way, hop - 1, piece)

        def some(i, carry):
            made = []
            for q in [i * GROUP + k for k in range(GROUP)]:
                total = own(n, q, held, way if held is other_next else 0)
                if onward:
                    total = total + read(way, hop - 1, q)
                top = jnp.max(jnp.abs(total), axis=0, keepdims=True)
                usable = top > 1e-30
                factor = jnp.where(usable, 32767.0 / jnp.where(usable, top, 1.0), 0.0)
                value = jnp.round(total * factor).astype(jnp.int32).astype(jnp.int16)
                made.append((q, value, top * (1.0 / 32767.0)))
            for q, value, scale in made:
                sent[way, hop, q] = value
                sent_scale[way, hop, pl.ds(q, 1), :] = scale
            return carry

        lax.fori_loop(piece * size // GROUP, (piece + 1) * size // GROUP, some, 0)
        for copy in ring(way, hop, piece):
            copy.start()

    def first(way):
        return range(PIECES // 2) if way == 0 else range(PIECES // 2, PIECES)

    wide = lax.broadcasted_iota(jnp.int32, (width, width), 1)
    tall = lax.broadcasted_iota(jnp.int32, (width, width), 0)

    def pivot(j, carry):
        old = a[...]
        row_a, row_v = a[pl.ds(j, 1), :], v[pl.ds(j, 1), :]
        d = jnp.sum(jnp.where(wide[:1] == j, row_a, 0.0), axis=1, keepdims=True)
        column = jnp.sum(jnp.where(wide == j, old, 0.0), axis=1, keepdims=True)
        factor = jnp.where(tall > j, column / d, 0.0)
        a[...] = old - factor * row_a
        v[...] = v[...] - factor * row_v
        return carry

    across(*early[0]).wait_recv()
    for way in range(2):
        for piece in first(way):
            send(way, 0, piece, False, other_far)
    gram_round(0)
    for n, to in early[1:]:
        across(n, to).wait_recv()
    turn = 1
    for piece in range(PIECES):
        for way in range(2):
            at = PIECES - 1 - piece if way == 0 else piece
            send(way, 1, at, at in first(way), other_next)
            if turn < rounds:
                gram_round(turn)
                turn += 1
    while turn < rounds:
        gram_round(turn)
        turn += 1
    a[...] = grams[rounds]
    v[...] = jnp.where(wide == tall, 1.0, 0.0)
    rest(lambda copy: copy.wait_recv())
    points = (half - 2) * PIECES * 2
    each = width // points
    lead = width - each * points
    lax.fori_loop(0, lead, pivot, 0)

    def onward(hop, carry):
        for piece in range(PIECES):
            for way in range(2):
                send(way, hop, PIECES - 1 - piece if way == 0 else piece, True)
                start = lead + (((hop - 2) * PIECES + piece) * 2 + way) * each
                lax.fori_loop(start, start + each, pivot, 0)
        return carry

    lax.fori_loop(2, half, onward, 0)

    d = jnp.sum(jnp.where(wide == tall, a[...], 0.0), axis=1, keepdims=True)
    inverse = v[...] / jnp.sqrt(d)
    spread = jnp.sum(jnp.where(wide == tall, grams[rounds], 0.0), axis=0, keepdims=True)
    grown = jnp.sum(inverse * inverse * spread, axis=1, keepdims=True)
    gain[...] = jnp.broadcast_to(jnp.sum(grown, axis=0, keepdims=True), gain.shape)
    high = inverse.astype(jnp.bfloat16)
    low = (inverse - high.astype(jnp.float32)).astype(jnp.bfloat16)
    factors[...] = jnp.concatenate(
        [
            jnp.concatenate([high, high], axis=1),
            jnp.concatenate([low, jnp.zeros_like(low)], axis=1),
        ],
        axis=0,
    )

    for piece in range(PIECES):
        for way in range(2):
            await_piece(way, half - 1, piece)

        def some(i, carry):
            made = []
            for q in [i * GROUP + k for k in range(GROUP)]:
                made.append((q, own(0, q) + read(0, half - 1, q) + read(1, half - 1, q)))
            for q, value in made:
                z_buf[pl.ds(pl.multiple_of(q * BLOCK, BLOCK), BLOCK), :] = value
            return carry

        lax.fori_loop(piece * size // GROUP, (piece + 1) * size // GROUP, some, 0)

        def product(i, carry):
            at = pl.ds(pl.multiple_of(i * 256, 256), 256)
            value = z_buf[at, :]
            top = value.astype(jnp.bfloat16)
            left = (value - top.astype(jnp.float32)).astype(jnp.bfloat16)
            two = lax.dot_general(
                jnp.concatenate([top, left], axis=1), factors[...], (((1,), (1,)), ((), ())),
                preferred_element_type=jnp.float32,
            )
            out[at, :] = (two[:, :width] + two[:, width:]).astype(out.dtype)
            return carry

        per = size * BLOCK // 256
        lax.fori_loop(piece * per, (piece + 1) * per, product, 0)

    def finish(way, hop, piece):
        for copy in ring(way, hop, piece):
            copy.wait_send()

    for way in range(2):
        for piece in first(way):
            finish(way, 0, piece)

    def finish_all(hop, carry):
        for piece in range(PIECES):
            for way in range(2):
                finish(way, hop, piece)
        return carry

    lax.fori_loop(1, half, finish_all, 0)
    for n, to in early:
        across(n, to).wait_send()
    rest(lambda copy: copy.wait_send())
    for i in range(rounds):
        gram_copy(i).wait_send()


def give_back(chips, cap, count, parts, gram, mine, theirs):
    edge, width = parts.shape[1:]
    half = chips // 2
    rounds = (2 * chips).bit_length() - 1
    dma = pltpu.SemaphoreType.DMA
    smem = pl.BlockSpec(memory_space=pltpu.SMEM)
    vmem = pl.BlockSpec(memory_space=pltpu.VMEM)
    f32 = jnp.float32
    return pl.pallas_call(
        functools.partial(return_kernel, chips, cap, rounds),
        out_shape=[
            jax.ShapeDtypeStruct((count * edge, width), jnp.bfloat16),
            jax.ShapeDtypeStruct((8, width), f32),
        ],
        in_specs=[vmem, vmem, smem, smem],
        out_specs=[vmem, vmem],
        scratch_shapes=[
            pltpu.VMEM((1, cap + 1, edge, width), f32),
            pltpu.VMEM((2, cap + 1, edge, width), f32),
            pltpu.VMEM((chips, cap + 1, edge, width), f32),
            pltpu.VMEM((2, half, count, edge, width), jnp.int16),
            pltpu.VMEM((2, half, count, edge, width), jnp.int16),
            pltpu.VMEM((2, half, count, width), f32),
            pltpu.VMEM((2, half, count, width), f32),
            pltpu.VMEM((rounds + 1, width, width), f32),
            pltpu.VMEM((rounds, width, width), f32),
            pltpu.VMEM((width, width), f32),
            pltpu.VMEM((width, width), f32),
            pltpu.VMEM((2 * width, 2 * width), jnp.bfloat16),
            pltpu.VMEM((count * edge, width), f32),
            dma((chips,)),
            dma((chips,)),
            dma((2, half, PIECES)),
            dma((2, half, PIECES)),
            dma((2, half, PIECES)),
            dma((2, half, PIECES)),
            dma((rounds,)),
            dma((rounds,)),
        ],
        compiler_params=pltpu.CompilerParams(
            collective_id=1, has_side_effects=True, vmem_limit_bytes=56 * 1024 * 1024
        ),
    )(parts, gram, mine, theirs)


def factor_of(sketch):
    local_gram = jnp.dot(sketch.T, sketch, precision=lax.Precision.HIGHEST)
    gram = lax.psum(local_gram, ("grp", "pan"))
    return jnp.linalg.cholesky(gram)


def careful(jblocks, blk_row, blk_src, blk_slot, live_count, send_list, omega):
    block_count = jblocks.shape[0]
    width = omega.shape[1]
    groups = lax.axis_size("grp")
    lists = send_list.reshape(-1)
    slots = lists.shape[0]
    cap = slots // groups
    edge = BLOCK
    cell_blocks = omega.shape[0] // edge
    alive = jnp.arange(block_count, dtype=jnp.int32) < live_count[0]
    values = jnp.where(alive[:, None], jblocks, jnp.zeros((), jblocks.dtype)).reshape(
        block_count, edge, edge
    )
    omega_blocks = omega.reshape(cell_blocks, edge, width)
    outgoing = jnp.take(omega_blocks, lists, axis=0).reshape(groups, cap * edge, width)
    incoming = lax.all_to_all(outgoing, "grp", split_axis=0, concat_axis=0, tiled=True).reshape(
        slots, edge, width
    )
    slot_index = blk_src * cap + blk_slot
    picked = jnp.take(incoming, slot_index, axis=0)
    products = jnp.einsum("bij,bjk->bik", values, picked, preferred_element_type=jnp.float32)
    sketch = jax.ops.segment_sum(products, blk_row, num_segments=RB_DEV)
    sketch = sketch.reshape(RB_DEV * edge, width)
    lower = factor_of(sketch)
    used_rows = lax.linalg.triangular_solve(lower, sketch.T, left_side=True, lower=True).T
    chosen = jnp.take(used_rows.reshape(RB_DEV, edge, width), blk_row, axis=0)
    terms = jnp.einsum(
        "bij,bik->bjk",
        values.astype(jnp.float32),
        chosen,
        precision=lax.Precision.HIGH,
        preferred_element_type=jnp.float32,
    )
    per_slot = terms[:slots].at[slot_index[slots:]].add(terms[slots:])
    returned = lax.all_to_all(
        per_slot.reshape(groups, cap * edge, width), "grp", split_axis=0, concat_axis=0, tiled=True
    )
    empty = jnp.zeros((cell_blocks, edge, width), jnp.float32)
    summed = empty.at[lists].add(returned.reshape(slots, edge, width))
    summed = summed.reshape(cell_blocks * edge, width)
    return summed.astype(jnp.bfloat16)


def per_device(jblocks, blk_row, blk_src, blk_slot, live_count, send_list, omega):
    blocks = jblocks.shape[0]
    chips, cap = lax.axis_size("grp") // 2, send_list.shape[-1]
    width = omega.shape[1]
    first = 2 * chips * cap
    count = omega.shape[0] // BLOCK
    listed = jnp.pad(send_list[0, 0].T, ((0, 0), (0, width - 2 * chips)))
    gathered, lists = gather(chips, omega, listed)
    x = jblocks.reshape(blocks, BLOCK // 2, 2 * BLOCK)
    parts, gram, my_at, their_at = local(first, lists, blk_row, blk_src, blk_slot, live_count, x, gathered)
    gram = sum_over("pan", lax.axis_size("pan"), gram)
    projected, gain = give_back(chips, cap, count, parts, gram, my_at, their_at)
    return lax.cond(
        gain[0, 0] <= MOST_GAIN * width,
        lambda *given: projected,
        careful,
        jblocks, blk_row, blk_src, blk_slot, live_count, send_list, omega,
    )


def solution(mesh):
    placed = (
        P(("grp", "pan"), None),
        P(("grp", "pan")),
        P(("grp", "pan")),
        P(("grp", "pan")),
        P(("grp", "pan")),
        P("grp", "pan", None, None),
        P(("grp", "pan"), None),
    )
    return jax.shard_map(
        per_device, mesh=mesh, in_specs=placed, out_specs=P(("grp", "pan"), None), check_vma=False
    )
```
